32 devices in a mesh: dp: 8 (over z, y), mp: 4 (over x, core).
Axes of the slice: x: 2, y: 2, z: 4, core: 2. Of those that a mesh axis runs over, the one named last changes fastest.
Arguments:
- tokens: bfloat16 [10240, 1024], P(('dp', 'mp')), may hold values from -6 to 6
- cotangent: bfloat16 [10240, 1024], P(('dp', 'mp')), may hold values from -6 to 6
- in_gain: float32 [2, 1024], replicated, may hold values from 0.1 to 1.9
- w_z: bfloat16 [2, 1024, 2048], P(None, 'dp', 'mp'), may hold values from -0.1875 to 0.1875
- w_x: bfloat16 [2, 1024, 2048], P(None, 'dp', 'mp'), may hold values from -0.1875 to 0.1875
- w_bc: bfloat16 [2, 1024, 256], P(None, 'dp'), may hold values from -0.1875 to 0.1875
- w_dt: bfloat16 [2, 1024, 32], P(None, 'dp', 'mp'), may hold values from -0.1875 to 0.1875
- conv_x_w: float32 [2, 4, 2048], P(None, None, 'mp'), may hold values from -3 to 3
- conv_x_b: float32 [2, 2048], P(None, 'mp'), may hold values from -3 to 3
- conv_bc_w: float32 [2, 4, 256], replicated, may hold values from -3 to 3
- conv_bc_b: float32 [2, 256], replicated, may hold values from -3 to 3
- dt_bias: float32 [2, 32], P(None, 'mp'), may hold values from -6.9 to -2.25
- a_log: float32 [2, 32], P(None, 'mp'), may hold values from 0 to 2.77
- dskip: float32 [2, 32], P(None, 'mp'), may hold values from 0.5 to 1.5
- norm_gain: float32 [2, 2048], P(None, 'mp'), may hold values from 0.1 to 1.9
- w_out: bfloat16 [2, 2048, 1024], P(None, 'mp', 'dp'), may hold values from -0.125 to 0.125
Outputs:
- outputs: float32 [10240, 1024], P(('dp', 'mp'))
- d_tokens: float32 [10240, 1024], P(('dp', 'mp'))
- g_in_gain: float32 [2, 1024], replicated
- g_w_z: float32 [2, 1024, 2048], P(None, 'dp', 'mp')
- g_w_x: float32 [2, 1024, 2048], P(None, 'dp', 'mp')
- g_w_bc: float32 [2, 1024, 256], P(None, 'dp')
- g_w_dt: float32 [2, 1024, 32], P(None, 'dp', 'mp')
- g_conv_x_w: float32 [2, 4, 2048], P(None, None, 'mp')
- g_conv_x_b: float32 [2, 2048], P(None, 'mp')
- g_conv_bc_w: float32 [2, 4, 256], replicated
- g_conv_bc_b: float32 [2, 256], replicated
- g_dt_bias: float32 [2, 32], P(None, 'mp')
- g_a_log: float32 [2, 32], P(None, 'mp')
- g_dskip: float32 [2, 32], P(None, 'mp')
- g_norm_gain: float32 [2, 2048], P(None, 'mp')
- g_w_out: float32 [2, 2048, 1024], P(None, 'mp', 'dp')
The draws below stay inside these ranges and needn't reach their ends.
All inputs are finite; a program needn't handle non-finite values.
Results may differ from the reference program's by a relative error of at most 0.0098.
Values may be sent and summed in bfloat16 or wider, within the bound.
A program may use at most 192 MiB of HBM per device.

```python
import jax
import jax.numpy as jnp
from jax import lax

D = 1024
INNER = 2048
HEADS = 32
HEADDIM = 64
STATE = 128
CONV = 4
SPAN = 256
LAYERS = 2
LEN = 1280
SEQS = 1
TOKENS = 10240


def head_classes(key, share):
    base = jax.random.fold_in(key, 101)
    layer_keys = jax.random.split(base, LAYERS)
    orders = jax.vmap(lambda item: jax.random.permutation(item, HEADS))(layer_keys)
    return (orders < share).astype(jnp.float32)


def draw_dt_bias(key, part):
    slow_heads = head_classes(key, HEADS // 2)
    key = jax.random.fold_in(key, 7)
    slow_values = jax.random.uniform(jax.random.fold_in(key, 1), (LAYERS, HEADS), jnp.float32, -6.9, -6.5)
    fast_values = jax.random.uniform(jax.random.fold_in(key, 2), (LAYERS, HEADS), jnp.float32, -4.5, -2.25)
    return slow_heads * slow_values + (1.0 - slow_heads) * fast_values


def draw_a_log(key, part):
    slow_heads = head_classes(key, HEADS // 2)
    key = jax.random.fold_in(key, 11)
    slow_values = jax.random.uniform(jax.random.fold_in(key, 1), (LAYERS, HEADS), jnp.float32, 0.0, 0.2)
    fast_values = jax.random.uniform(jax.random.fold_in(key, 2), (LAYERS, HEADS), jnp.float32, 0.0, 2.77)
    return slow_heads * slow_values + (1.0 - slow_heads) * fast_values


def steps_of(stream_key, dims, cuts, low, largest):
    def one(dim, parts):
        draws = jax.random.uniform(jax.random.fold_in(jax.random.fold_in(stream_key, 6), dim), (parts,), jnp.float32, low / len(cuts), largest / len(cuts))
        return jnp.repeat(jnp.exp(draws), dims[dim] // parts).reshape((-1,) + (1,) * (len(dims) - dim - 1))

    level = one(*cuts[0])
    for cut in cuts[1:]:
        level = level * one(*cut)
    return level


def centred(key, shape, spread, bound, cuts=(), held_as=jnp.bfloat16):
    array = spread * jax.random.normal(key, shape, jnp.float32)
    if cuts:
        array = array * steps_of(key, shape, cuts, -0.22, 0.18)
    return jnp.clip(array, -bound, bound).astype(held_as)


def setup_inputs(seed: int = 0) -> dict:
    key_list = jax.random.split(jax.random.key(seed), 17)
    return {
        "tokens": centred(key_list[0], (TOKENS, D), 1.0, 6.0, ((0, 32),)),
        "cotangent": centred(key_list[1], (TOKENS, D), 1.0, 6.0, ((0, 32),)),
        "in_gain": jnp.clip(1.0 + 0.18 * jax.random.normal(key_list[2], (LAYERS, D), jnp.float32), 0.1, 1.9),
        "w_z": centred(key_list[3], (LAYERS, D, INNER), D ** -0.5, 0.1875, ((1, 8), (2, 4))),
        "w_x": centred(key_list[4], (LAYERS, D, INNER), D ** -0.5, 0.1875, ((1, 8), (2, 4))),
        "w_bc": centred(key_list[5], (LAYERS, D, 2 * STATE), D ** -0.5, 0.1875, ((1, 8),)),
        "w_dt": centred(key_list[6], (LAYERS, D, HEADS), D ** -0.5, 0.1875, ((1, 8), (2, 4))),
        "conv_x_w": centred(key_list[7], (LAYERS, CONV, INNER), CONV ** -0.5, 3.0, ((2, 4),), jnp.float32),
        "conv_x_b": centred(key_list[8], (LAYERS, INNER), 0.5, 3.0, ((1, 4),), jnp.float32),
        "conv_bc_w": centred(key_list[9], (LAYERS, CONV, 2 * STATE), CONV ** -0.5, 3.0, (), jnp.float32),
        "conv_bc_b": centred(key_list[10], (LAYERS, 2 * STATE), 0.5, 3.0, (), jnp.float32),
        "dt_bias": draw_dt_bias(jax.random.fold_in(key_list[16], 71), 0),
        "a_log": draw_a_log(jax.random.fold_in(key_list[16], 71), 0),
        "dskip": jnp.clip(0.5 + 1.0 * jax.random.uniform(key_list[13], (LAYERS, HEADS), jnp.float32) ** steps_of(key_list[13], (LAYERS, HEADS), ((1, 4),), -0.2, 0.2), 0.5, 1.5),
        "norm_gain": jnp.clip(1.0 + 0.18 * jax.random.normal(key_list[14], (LAYERS, INNER), jnp.float32), 0.1, 1.9),
        "w_out": centred(key_list[15], (LAYERS, INNER, D), INNER ** -0.5, 0.125, ((1, 4), (2, 8))),
    }


epsilon = 1e-05
HIGHEST_PRECISION = lax.Precision.HIGHEST

@jax.custom_vjp
def low(v):
    return lax.optimization_barrier(v.astype(jnp.bfloat16)).astype(jnp.float32)

@jax.custom_vjp
def low_back(v):
    return v

def low_keep(v):
    return (low(v), None)

def low_pass(kept, grad):
    return (grad,)

def back_keep(v):
    return (v, None)

def back_low(kept, grad):
    return (low(grad),)
low.defvjp(low_keep, low_pass)
low_back.defvjp(back_keep, back_low)

def causal_conv(values, kernel, offset, seq_len):
    rows, width = values.shape
    taps = kernel.shape[0]
    seqs = values.reshape(rows // seq_len, seq_len, width)
    padded = jnp.pad(seqs, ((0, 0), (taps - 1, 0), (0, 0)))
    summed = offset + jnp.zeros_like(seqs)
    for shift_tap in range(taps):
        summed = summed + padded[:, shift_tap:shift_tap + seq_len, :] * kernel[shift_tap]
    return jax.nn.silu(summed).reshape(rows, width)

def span_step(rate, state, block):
    inputs, steps, keys, reads = block
    logs = jnp.cumsum(steps * rate, axis=1)
    heads_first = jnp.swapaxes(logs, 1, 2)
    differ = heads_first[:, :, :, None] - heads_first[:, :, None, :]
    length = logs.shape[1]
    lower = jnp.arange(length)[:, None] >= jnp.arange(length)[None, :]
    decays = jnp.exp(jnp.where(lower, differ, -1e+30))
    scores = jnp.einsum('sin,sjn->sij', reads, keys, precision=HIGHEST_PRECISION)
    weights = scores[:, None] * decays * jnp.swapaxes(steps, 1, 2)[:, :, None, :]
    inner_out = jnp.einsum('shij,sjhp->sihp', weights, inputs, precision=HIGHEST_PRECISION)
    carried = jnp.einsum('sin,shnp->sihp', reads, state, precision=HIGHEST_PRECISION) * jnp.exp(logs)[..., None]
    last_log = logs[:, -1, :]
    tails = jnp.exp(last_log[:, None, :] - logs) * steps
    update = jnp.einsum('sjn,sjhp->shnp', keys, inputs * tails[..., None], precision=HIGHEST_PRECISION)
    new_state = state * jnp.exp(last_log)[:, :, None, None] + update
    return (new_state, inner_out + carried)

def state_scan(inputs, steps, rate, keys, reads):
    rows = inputs.shape[0]
    heads = steps.shape[1]
    seqs = rows // LEN
    count = LEN // SPAN

    def split_blocks(value):
        value = value.reshape((seqs, count, SPAN) + value.shape[1:])
        return jnp.moveaxis(value, 1, 0)
    blocks = (split_blocks(inputs.reshape(rows, heads, HEADDIM)), split_blocks(steps), split_blocks(keys), split_blocks(reads))
    start_state = jnp.zeros((seqs, heads, STATE, HEADDIM), jnp.float32)
    step_fn = jax.checkpoint(lambda state, block: span_step(rate, state, block))
    final_state, outs = lax.scan(step_fn, start_state, blocks)
    return jnp.moveaxis(outs, 0, 1).reshape(rows, heads * HEADDIM)

def mixer_part(x_raw, bc_act, dt_raw, conv_w, conv_b, dt_off, log_rate, skip_coef):
    x_act = causal_conv(x_raw, conv_w, conv_b, LEN)
    steps = jax.nn.softplus(dt_raw + dt_off)
    scanned = state_scan(x_act, steps, -jnp.exp(log_rate), bc_act[:, :STATE], bc_act[:, STATE:])
    return scanned + x_act * jnp.repeat(skip_coef, HEADDIM)

def layer(current, params):
    in_gain, w_z, w_x, w_bc, w_dt, conv_x_w, conv_x_b, conv_bc_w, conv_bc_b, dt_bias, a_log, dskip, norm_gain, w_out = params
    scale = lax.rsqrt(lax.optimization_barrier(jnp.mean(current * current, axis=-1, keepdims=True)) + epsilon)
    normed = low(current * scale * in_gain)
    z_val = low_back(jnp.dot(normed, w_z, precision=HIGHEST_PRECISION))
    x_raw = low_back(jnp.dot(normed, w_x, precision=HIGHEST_PRECISION))
    bc_raw = low_back(jnp.dot(normed, w_bc, precision=HIGHEST_PRECISION))
    dt_raw = low_back(jnp.dot(normed, w_dt, precision=HIGHEST_PRECISION))
    bc_act = causal_conv(bc_raw, conv_bc_w, conv_bc_b, LEN)
    mixed_y = mixer_part(x_raw, bc_act, dt_raw, conv_x_w, conv_x_b, dt_bias, a_log, dskip)
    gated = mixed_y * jax.nn.silu(z_val)
    ratio = lax.rsqrt(lax.optimization_barrier(jnp.mean(gated * gated, axis=-1, keepdims=True)) + epsilon)
    mixed = low(gated * ratio * norm_gain)
    branch = low_back(jnp.dot(mixed, w_out, precision=HIGHEST_PRECISION))
    return current + branch

def reference(tokens, cotangent, in_gain, w_z, w_x, w_bc, w_dt, conv_x_w, conv_x_b, conv_bc_w, conv_bc_b, dt_bias, a_log, dskip, norm_gain, w_out):
    params = tuple((value.astype(jnp.float32) for value in (in_gain, w_z, w_x, w_bc, w_dt, conv_x_w, conv_x_b, conv_bc_w, conv_bc_b, dt_bias, a_log, dskip, norm_gain, w_out)))
    group_rows = SEQS * LEN
    groups = tokens.shape[0] // group_rows
    inputs_all = tokens.astype(jnp.float32).reshape(groups, group_rows, D)
    cotan_all = cotangent.astype(jnp.float32).reshape(groups, group_rows, D)

    def forward(current, weights):
        for depth in range(LAYERS):
            current = layer(current, tuple((value[depth] for value in weights)))
        return current

    def group_step(totals, item):
        current, cotan = item
        result, pullback = jax.vjp(forward, current, params)
        d_input, d_params = pullback(cotan)
        return (tuple((first + second for first, second in zip(totals, d_params))), (result, d_input))
    zeros = tuple((jnp.zeros_like(value) for value in params))
    totals, (results, d_inputs) = lax.scan(group_step, zeros, (inputs_all, cotan_all))
    return (results.reshape(-1, D), d_inputs.reshape(-1, D), totals[0], totals[1], totals[2], totals[3], totals[4], totals[5], totals[6], totals[7], totals[8], totals[9], totals[10], totals[11], totals[12], totals[13])
```

```python
import functools

import jax
import jax.numpy as jnp
from jax import lax
from jax.experimental import pallas as pl
from jax.experimental.pallas import tpu as pltpu
from jax.sharding import PartitionSpec as P

INNER = 2048
HEADDIM = 64
STATE = 128
SPAN = 256
LEN = 1280
PAIR = 2 * HEADDIM
LANES = 128

epsilon = 1e-05
HIGHEST = lax.Precision.HIGHEST
F32 = jnp.float32
BF16 = jnp.bfloat16


def contract(left, right, dims):
    return lax.dot_general(left, right, (dims, ((), ())), preferred_element_type=F32)


NN = ((1,), (0,))
NT = ((1,), (1,))
TN = ((0,), (0,))


def causal_conv(values, kernel, offset):
    rows, width = values.shape
    taps = kernel.shape[0]
    seqs = values.reshape(rows // LEN, LEN, width)
    padded = jnp.pad(seqs, ((0, 0), (taps - 1, 0), (0, 0)))
    summed = offset + jnp.zeros_like(seqs)
    for tap in range(taps):
        summed = summed + padded[:, tap : tap + LEN, :] * kernel[tap]
    return jax.nn.silu(summed).reshape(rows, width)


def pair_masks():
    lane = lax.broadcasted_iota(jnp.int32, (1, PAIR), 1)
    first = lane < HEADDIM
    return first, jnp.logical_not(first)


def lower_mask():
    row = lax.broadcasted_iota(jnp.int32, (SPAN, SPAN), 0)
    col = lax.broadcasted_iota(jnp.int32, (SPAN, SPAN), 1)
    return row >= col


def scan_forward(heads, x_ref, b_ref, c_ref, dt_ref, dtt_ref, l_ref, lt_ref, skip_ref, y_ref, h_ref, state):
    @pl.when(pl.program_id(1) == 0)
    def _():
        state[...] = jnp.zeros_like(state)

    h_ref[0] = state[...]
    keys = b_ref[...].astype(BF16)
    reads = c_ref[...].astype(BF16)
    scores = contract(reads, keys, NT)
    lower = lower_mask()
    masks = pair_masks()
    for pair in range(heads // 2):
        lanes = slice(pair * PAIR, (pair + 1) * PAIR)
        x = x_ref[:, lanes]
        held = state[:, lanes]
        inner = None
        grown, tails, shrink = [], [], []
        for k in range(2):
            h = 2 * pair + k
            l_col = l_ref[:, h : h + 1]
            last = l_ref[SPAN - 1 : SPAN, h : h + 1]
            decay = jnp.exp(jnp.where(lower, l_col - lt_ref[h : h + 1, :], -1e30))
            weights = (scores * decay * dtt_ref[h : h + 1, :]).astype(BF16)
            part = contract(weights, jnp.where(masks[k], x, 0.0).astype(BF16), NN)
            inner = part if inner is None else inner + part
            grown.append(jnp.exp(l_col))
            tails.append(jnp.exp(last - l_col) * dt_ref[:, h : h + 1])
            shrink.append(jnp.exp(last))
        carried = contract(reads, held.astype(BF16), NN) * jnp.where(masks[0], grown[0], grown[1])
        y_ref[:, lanes] = inner + carried + x * skip_ref[:, lanes]
        scaled = (x * jnp.where(masks[0], tails[0], tails[1])).astype(BF16)
        state[:, lanes] = held * jnp.where(masks[0], shrink[0], shrink[1]) + contract(keys, scaled, TN)


def scan_backward(
    heads,
    x_ref, b_ref, c_ref, dt_ref, dtt_ref, l_ref, lt_ref, skip_ref, h_ref, dy_ref,
    dx_ref, db_ref, dc_ref, dl_ref, ddt_ref, col_ref, xdy_ref,
    d_state,
):
    @pl.when(pl.program_id(1) == 0)
    def _():
        d_state[...] = jnp.zeros_like(d_state)

    keys = b_ref[...].astype(BF16)
    reads = c_ref[...].astype(BF16)
    scores = contract(reads, keys, NT)
    lower = lower_mask()
    masks = pair_masks()
    head_lane = lax.broadcasted_iota(jnp.int32, (1, heads), 1)
    is_last = lax.broadcasted_iota(jnp.int32, (SPAN, 1), 0) == SPAN - 1
    d_scores = jnp.zeros((SPAN, SPAN), F32)
    d_keys = jnp.zeros((SPAN, STATE), F32)
    d_reads = jnp.zeros((SPAN, STATE), F32)
    d_logs = jnp.zeros((SPAN, heads), F32)
    d_steps = jnp.zeros((SPAN, heads), F32)
    x_dy = jnp.zeros((SPAN, heads), F32)
    for pair in range(heads // 2):
        lanes = slice(pair * PAIR, (pair + 1) * PAIR)
        x = x_ref[:, lanes]
        dy = dy_ref[:, lanes]
        held = h_ref[0, :, lanes]
        d_held = d_state[:, lanes]
        l_cols = [l_ref[:, 2 * pair + k : 2 * pair + k + 1] for k in range(2)]
        lasts = [l_ref[SPAN - 1 : SPAN, 2 * pair + k : 2 * pair + k + 1] for k in range(2)]
        dt_cols = [dt_ref[:, 2 * pair + k : 2 * pair + k + 1] for k in range(2)]
        rests = [jnp.exp(lasts[k] - l_cols[k]) for k in range(2)]
        shrink = [jnp.exp(lasts[k]) for k in range(2)]
        grown = jnp.where(masks[0], jnp.exp(l_cols[0]), jnp.exp(l_cols[1]))
        tails = jnp.where(masks[0], rests[0] * dt_cols[0], rests[1] * dt_cols[1])
        x_low = x.astype(BF16)
        held_low = held.astype(BF16)
        d_held_low = d_held.astype(BF16)
        outer = dy * grown
        outer_low = outer.astype(BF16)
        from_logs = outer * contract(reads, held_low, NN)
        d_reads = d_reads + contract(outer_low, held_low, NT)
        carried = contract(keys, d_held_low, NN)
        from_tails = x * carried
        d_keys = d_keys + contract((x * tails).astype(BF16), d_held_low, NT)
        x_times_dy = x * dy
        d_x = tails * carried + skip_ref[:, lanes] * dy
        kept = jnp.sum(held * d_held, axis=0, keepdims=True)
        for k in range(2):
            h = 2 * pair + k
            step_row = dtt_ref[h : h + 1, :]
            decay = jnp.exp(jnp.where(lower, l_cols[k] - lt_ref[h : h + 1, :], -1e30))
            scored = scores * decay
            dy_low = jnp.where(masks[k], dy, 0.0).astype(BF16)
            d_weights = contract(dy_low, x_low, NT)
            d_x = d_x + contract((scored * step_row).astype(BF16), dy_low, TN)
            product = d_weights * scored
            d_scores = d_scores + d_weights * decay * step_row
            col_ref[0, h : h + 1, :] = jnp.sum(product, axis=0, keepdims=True)
            row_sum = jnp.sum(product * step_row, axis=1, keepdims=True)
            log_sum = jnp.sum(jnp.where(masks[k], from_logs, 0.0), axis=1, keepdims=True)
            tail_sum = jnp.sum(jnp.where(masks[k], from_tails, 0.0), axis=1, keepdims=True)
            skip_sum = jnp.sum(jnp.where(masks[k], x_times_dy, 0.0), axis=1, keepdims=True)
            step_part = tail_sum * rests[k]
            tail_part = step_part * dt_cols[k]
            ending = shrink[k] * jnp.sum(jnp.where(masks[k], kept, 0.0), axis=1, keepdims=True) + jnp.sum(
                tail_part, axis=0, keepdims=True
            )
            log_part = log_sum + row_sum - tail_part + jnp.where(is_last, ending, 0.0)
            here = head_lane == h
            d_logs = jnp.where(here, log_part, d_logs)
            d_steps = jnp.where(here, step_part, d_steps)
            x_dy = jnp.where(here, skip_sum, x_dy)
        dx_ref[:, lanes] = d_x
        d_state[:, lanes] = d_held * jnp.where(masks[0], shrink[0], shrink[1]) + contract(reads, outer_low, TN)
    d_scores_low = d_scores.astype(BF16)
    dc_ref[...] = d_reads + contract(d_scores_low, keys, NN)
    db_ref[...] = d_keys + contract(d_scores_low, reads, TN)
    dl_ref[...] = d_logs
    ddt_ref[...] = d_steps
    xdy_ref[...] = x_dy


def scan_specs(rows, width, heads, backward):
    count = LEN // SPAN

    def at(seq, step):
        return seq * count + ((count - 1 - step) if backward else step)

    def rowwise(columns, column=0):
        return pl.BlockSpec((SPAN, columns), lambda s, i: (at(s, i), column))

    def stacked(first, second):
        return pl.BlockSpec((1, first, second), lambda s, i: (at(s, i), 0, 0))

    across = pl.BlockSpec((heads, SPAN), lambda s, i: (0, at(s, i)))
    whole = pl.BlockSpec((1, width), lambda s, i: (0, 0))
    operands = [rowwise(width), rowwise(STATE, 0), rowwise(STATE, 1), rowwise(heads), across, rowwise(heads), across, whole]
    return operands, rowwise, stacked, (rows // LEN, count)


PARAMS = pltpu.CompilerParams(
    dimension_semantics=("arbitrary", "arbitrary"), vmem_limit_bytes=40 * 1024 * 1024
)


def run_forward(x, bc, steps, logs, skip):
    rows, width = x.shape
    heads = steps.shape[1]
    operands, rowwise, stacked, grid = scan_specs(rows, width, heads, False)
    blocks = rows // SPAN
    return pl.pallas_call(
        functools.partial(scan_forward, heads),
        grid=grid,
        in_specs=operands,
        out_specs=[rowwise(width), stacked(STATE, width)],
        out_shape=[
            jax.ShapeDtypeStruct((rows, width), F32),
            jax.ShapeDtypeStruct((blocks, STATE, width), F32),
        ],
        scratch_shapes=[pltpu.VMEM((STATE, width), F32)],
        compiler_params=PARAMS,
        cost_estimate=pl.CostEstimate(
            flops=blocks * heads * 4 * SPAN * SPAN * PAIR * 4, bytes_accessed=rows * width * 10, transcendentals=blocks * heads * SPAN * SPAN
        ),
        name="scan_forward",
    )(x, bc, bc, steps, steps.T, logs, logs.T, skip)


def run_backward(x, bc, steps, logs, skip, states, d_y):
    rows, width = x.shape
    heads = steps.shape[1]
    operands, rowwise, stacked, grid = scan_specs(rows, width, heads, True)
    blocks = rows // SPAN
    return pl.pallas_call(
        functools.partial(scan_backward, heads),
        grid=grid,
        in_specs=operands + [stacked(STATE, width), rowwise(width)],
        out_specs=[
            rowwise(width), rowwise(STATE), rowwise(STATE), rowwise(heads), rowwise(heads), stacked(heads, SPAN), rowwise(heads),
        ],
        out_shape=[
            jax.ShapeDtypeStruct((rows, width), F32),
            jax.ShapeDtypeStruct((rows, STATE), F32),
            jax.ShapeDtypeStruct((rows, STATE), F32),
            jax.ShapeDtypeStruct((rows, heads), F32),
            jax.ShapeDtypeStruct((rows, heads), F32),
            jax.ShapeDtypeStruct((blocks, heads, SPAN), F32),
            jax.ShapeDtypeStruct((rows, heads), F32),
        ],
        scratch_shapes=[pltpu.VMEM((STATE, width), F32)],
        compiler_params=PARAMS,
        cost_estimate=pl.CostEstimate(
            flops=blocks * heads * 12 * SPAN * SPAN * PAIR * 4, bytes_accessed=rows * width * 20, transcendentals=blocks * heads * SPAN * SPAN
        ),
        name="scan_backward",
    )(x, bc, bc, steps, steps.T, logs, logs.T, skip, states, d_y)


def block_sums(values, reverse):
    rows, heads = values.shape
    lower = jnp.tril(jnp.ones((SPAN, SPAN), F32))
    blocks = values.reshape(rows // SPAN, SPAN, heads)
    form = "ij,cih->cjh" if reverse else "ij,cjh->cih"
    return jnp.einsum(form, lower, blocks, precision=HIGHEST).reshape(rows, heads)


def swap_mp(value, bit, size):
    return lax.ppermute(value, "mp", [(i, i ^ bit) for i in range(size)])


def gather_mp(value):
    size = lax.axis_size("mp")
    if size != 4:
        return lax.all_gather(value, "mp", axis=0, tiled=True)
    chip, core = lax.axis_index("mp") // 2, lax.axis_index("mp") % 2
    far = swap_mp(value, 2, size)
    column = jnp.stack([jnp.where(chip == 0, value, far), jnp.where(chip == 0, far, value)])
    near = swap_mp(column, 1, size)
    both = jnp.stack([jnp.where(core == 0, column, near), jnp.where(core == 0, near, column)], axis=1)
    return both.reshape((size * value.shape[0],) + value.shape[1:])


def scatter_mp(value):
    size = lax.axis_size("mp")
    if size != 4:
        return lax.psum_scatter(value, "mp", scatter_dimension=0, tiled=True)
    chip, core = lax.axis_index("mp") // 2, lax.axis_index("mp") % 2
    parts = value.reshape(2, 2, value.shape[0] // size, value.shape[1])
    near = swap_mp(lax.dynamic_index_in_dim(parts, 1 - core, 1, False).astype(BF16), 1, size)
    column = lax.dynamic_index_in_dim(parts, core, 1, False) + near.astype(F32)
    far = swap_mp(lax.dynamic_index_in_dim(column, 1 - chip, 0, False).astype(BF16), 2, size)
    return lax.dynamic_index_in_dim(column, chip, 0, False) + far.astype(F32)


def sum_all(value, axis):
    size = lax.axis_size(axis)
    bit = 1
    while bit < size:
        value = value + lax.ppermute(value, axis, [(i, i ^ bit) for i in range(size)])
        bit *= 2
    return value


def reduce_line(parts, place, size, device):
    own = lax.dynamic_index_in_dim(parts, place, 0, False)
    for way in (1, -1):
        along = place if way == 1 else size - 1 - place
        sent = None
        for step in range(size - 1):
            target = jnp.clip(place + way * (size - 1 - step), 0, size - 1)
            part = lax.dynamic_index_in_dim(parts, target, 0, False)
            if sent is not None:
                part = part + sent.astype(F32)
            pairs = []
            for row in range(step + 1):
                here = row if way == 1 else size - 1 - row
                pairs += device(here, here + way)
            sent = lax.ppermute(part.astype(BF16), "dp", pairs)
        own = own + sent.astype(F32)
    return own


def scatter_dp(value):
    size = lax.axis_size("dp")
    if size != 8:
        return lax.psum_scatter(value, "dp", scatter_dimension=0, tiled=True)
    outer, inner = 4, 2
    parts = value.reshape(outer, inner, value.shape[0] // size, value.shape[1])
    index = lax.axis_index("dp")
    column = reduce_line(
        parts, index // inner, outer, lambda a, b: [(a * inner + i, b * inner + i) for i in range(inner)]
    )
    return reduce_line(
        column, index % inner, inner, lambda a, b: [(o * inner + a, o * inner + b) for o in range(outer)]
    )


def body(
    tokens, cotangent, in_gain, w_z, w_x, w_bc, w_dt, conv_x_w, conv_x_b, conv_bc_w, conv_bc_b, dt_bias, a_log, dskip, norm_gain, w_out,
):
    layers = w_z.shape[0]
    width = w_z.shape[2]
    heads = w_dt.shape[2]
    pair = w_bc.shape[2]
    inputs = 2 * width + pair + LANES
    pad_heads = ((0, 0), (0, LANES - heads))
    packed = []
    for depth in range(layers):
        own = jnp.concatenate(
            [w_z[depth], w_x[depth], w_bc[depth], jnp.pad(w_dt[depth], pad_heads), w_out[depth].T], axis=1
        )
        packed.append(
            tuple(lax.all_gather(part, "dp", axis=0, tiled=True) for part in (own[:, :inputs], own[:, inputs:]))
        )

    current = tokens.astype(F32)
    saved = []
    for depth in range(layers):
        w_in, w_down = packed[depth]
        scale = lax.rsqrt(jnp.mean(current * current, axis=-1, keepdims=True) + epsilon)
        normed = (current * scale * in_gain[depth]).astype(BF16)
        gathered = gather_mp(normed)
        raw = contract(gathered, w_in, NN)
        z_val = raw[:, :width]
        x_raw = raw[:, width : 2 * width]
        bc_raw = raw[:, 2 * width : 2 * width + pair]
        dt_in = raw[:, 2 * width + pair : 2 * width + pair + heads] + dt_bias[depth]
        x_act = causal_conv(x_raw, conv_x_w[depth], conv_x_b[depth])
        bc_act = causal_conv(bc_raw, conv_bc_w[depth], conv_bc_b[depth])
        steps = jax.nn.softplus(dt_in)
        rate = -jnp.exp(a_log[depth])
        logs = block_sums(steps * rate, False)
        skip = jnp.repeat(dskip[depth], HEADDIM)[None, :]
        mixed_y, states = run_forward(x_act, bc_act, steps, logs, skip)
        gated = mixed_y * jax.nn.silu(z_val)
        squares = lax.psum(jnp.sum(gated * gated, axis=-1), "mp")
        ratio = lax.rsqrt(squares / INNER + epsilon)[:, None]
        mixed = (gated * ratio * norm_gain[depth]).astype(BF16)
        branch = scatter_mp(contract(mixed, w_down, NT))
        saved.append((current, scale, gathered, raw, dt_in, x_act, bc_act, steps, rate, logs, skip, mixed_y, states, ratio, mixed))
        current = current + branch

    result = current
    gradient = cotangent.astype(F32)
    list_proj, list_own, list_shared = ([], [], [])
    for depth in reversed(range(layers)):
        current, scale, gathered, raw, dt_in, x_act, bc_act, steps, rate, logs, skip, mixed_y, states, ratio, mixed = saved[depth]
        w_in, w_down = packed[depth]
        z_val = raw[:, :width]
        x_raw = raw[:, width : 2 * width]
        bc_raw = raw[:, 2 * width : 2 * width + pair]
        grad_rows = gather_mp(gradient.astype(BF16))
        d_mixed = contract(grad_rows, w_down, NN)
        sigmoid_z = jax.nn.sigmoid(z_val)
        gate_act = z_val * sigmoid_z
        gated = mixed_y * gate_act
        weighted = d_mixed * norm_gain[depth]
        products = lax.psum(jnp.sum(weighted * gated, axis=-1), "mp")
        g_gain_norm = jnp.sum(d_mixed * gated * ratio, axis=0)
        d_gated = ratio * weighted - gated * ratio * ratio * ratio * (products / INNER)[:, None]
        d_y = d_gated * gate_act
        d_z = d_gated * mixed_y * sigmoid_z * (1.0 + z_val * (1.0 - sigmoid_z))
        z_low = d_z.astype(BF16)
        early = scatter_dp(jnp.concatenate([contract(gathered, z_low, TN), contract(grad_rows, mixed, TN)], axis=1))
        d_x, d_keys, d_reads, d_logs, d_steps, columns, x_dy = run_backward(x_act, bc_act, steps, logs, skip, states, d_y)
        columns = jnp.swapaxes(columns, 1, 2).reshape(steps.shape)
        d_ramps = block_sums(d_logs - steps * columns, True)
        g_alog = jnp.sum(steps * d_ramps, axis=0) * rate
        d_dtr = (d_steps + columns + rate * d_ramps) * jax.nn.sigmoid(dt_in)
        g_dtb = jnp.sum(d_dtr, axis=0)
        g_skip = jnp.sum(x_dy, axis=0)
        _, x_pull = jax.vjp(causal_conv, x_raw, conv_x_w[depth], conv_x_b[depth])
        _, bc_pull = jax.vjp(causal_conv, bc_raw, conv_bc_w[depth], conv_bc_b[depth])
        d_xr, g_cxw, g_cxb = x_pull(d_x)
        d_bcr, g_cbw, g_cbb = bc_pull(jnp.concatenate([d_keys, d_reads], axis=1))
        d_low = jnp.concatenate(
            [d_xr.astype(BF16), d_bcr.astype(BF16), jnp.pad(d_dtr.astype(BF16), pad_heads)], axis=1
        )
        d_normed = scatter_mp(contract(z_low, w_in[:, :width], NT) + contract(d_low, w_in[:, width:], NT))
        late = scatter_dp(contract(gathered, d_low, TN))
        list_proj.append((early[:, :width], late[:, :width], late[:, width : width + pair], late[:, width + pair : width + pair + heads], early[:, width:].T))
        gained = d_normed * in_gain[depth]
        g_gain_in = jnp.sum(d_normed * current * scale, axis=0)
        gradient = (
            gradient
            + scale * gained
            - current * scale * scale * scale * jnp.mean(gained * current, axis=-1, keepdims=True)
        )
        list_own.append((g_cxw, g_cxb, g_dtb, g_alog, g_skip, g_gain_norm))
        list_shared.append((g_cbw, g_cbb, g_gain_in))
    proj = [jnp.stack([entry[i] for entry in list_proj[::-1]]) for i in range(5)]
    own = [jnp.stack([entry[i] for entry in list_own[::-1]]) for i in range(6)]
    shared = [jnp.stack([entry[i] for entry in list_shared[::-1]]) for i in range(3)]
    sums = sum_all(jnp.concatenate([value.reshape(-1) for value in own + shared]), "dp")
    kept = sum(value.size for value in own)
    pieces, place = [], 0
    for value in own:
        pieces.append(sums[place : place + value.size].reshape(value.shape))
        place += value.size
    g_bc = proj[2]
    across = sum_all(jnp.concatenate([sums[kept:], g_bc.reshape(-1)]), "mp")
    place = 0
    for value in shared + [g_bc]:
        pieces.append(across[place : place + value.size].reshape(value.shape))
        place += value.size
    g_cxw, g_cxb, g_dtb, g_alog, g_skip, g_gain_norm, g_cbw, g_cbb, g_gain_in, g_bc = pieces
    return (
        result,
        gradient,
        g_gain_in,
        proj[0],
        proj[1],
        g_bc,
        proj[3],
        g_cxw,
        g_cxb,
        g_cbw,
        g_cbb,
        g_dtb,
        g_alog,
        g_skip,
        g_gain_norm,
        proj[4],
    )


def solution(mesh):
    placed = (
        P(("dp", "mp"), None),
        P(("dp", "mp"), None),
        P(),
        P(None, "dp", "mp"),
        P(None, "dp", "mp"),
        P(None, "dp", None),
        P(None, "dp", "mp"),
        P(None, None, "mp"),
        P(None, "mp"),
        P(),
        P(),
        P(None, "mp"),
        P(None, "mp"),
        P(None, "mp"),
        P(None, "mp"),
        P(None, "mp", "dp"),
    )
    return jax.shard_map(
        body,
        mesh=mesh,
        in_specs=placed,
        out_specs=placed[:1] * 2 + placed[2:],
        check_vma=False,
    )
```

```python
import functools

import jax
import jax.numpy as jnp
from jax import lax
from jax.experimental import pallas as pl
from jax.experimental.pallas import tpu as pltpu
from jax.sharding import PartitionSpec as P

INNER = 2048
HEADDIM = 64
STATE = 128
SPAN = 256
LEN = 1280
PAIR = 2 * HEADDIM
LANES = 128

epsilon = 1e-05
HIGHEST = lax.Precision.HIGHEST
F32 = jnp.float32
BF16 = jnp.bfloat16


def contract(left, right, dims):
    return lax.dot_general(left, right, (dims, ((), ())), preferred_element_type=F32)


NN = ((1,), (0,))
NT = ((1,), (1,))
TN = ((0,), (0,))


def causal_conv(values, kernel, offset):
    rows, width = values.shape
    taps = kernel.shape[0]
    seqs = values.reshape(rows // LEN, LEN, width)
    padded = jnp.pad(seqs, ((0, 0), (taps - 1, 0), (0, 0)))
    summed = offset + jnp.zeros_like(seqs)
    for tap in range(taps):
        summed = summed + padded[:, tap : tap + LEN, :] * kernel[tap]
    return jax.nn.silu(summed).reshape(rows, width)


def pair_masks():
    lane = lax.broadcasted_iota(jnp.int32, (1, PAIR), 1)
    first = lane < HEADDIM
    return first, jnp.logical_not(first)


def lower_mask():
    row = lax.broadcasted_iota(jnp.int32, (SPAN, SPAN), 0)
    col = lax.broadcasted_iota(jnp.int32, (SPAN, SPAN), 1)
    return row >= col


def scan_forward(heads, x_ref, b_ref, c_ref, dt_ref, dtt_ref, l_ref, lt_ref, skip_ref, y_ref, h_ref, state):
    @pl.when(pl.program_id(1) == 0)
    def _():
        state[...] = jnp.zeros_like(state)

    h_ref[0] = state[...]
    keys = b_ref[...].astype(BF16)
    reads = c_ref[...].astype(BF16)
    scores = contract(reads, keys, NT)
    lower = lower_mask()
    masks = pair_masks()
    for pair in range(heads // 2):
        lanes = slice(pair * PAIR, (pair + 1) * PAIR)
        x = x_ref[:, lanes]
        held = state[:, lanes]
        inner = None
        grown, tails, shrink = [], [], []
        for k in range(2):
            h = 2 * pair + k
            l_col = l_ref[:, h : h + 1]
            last = l_ref[SPAN - 1 : SPAN, h : h + 1]
            decay = jnp.exp(jnp.where(lower, l_col - lt_ref[h : h + 1, :], -1e30))
            weights = (scores * decay * dtt_ref[h : h + 1, :]).astype(BF16)
            part = contract(weights, jnp.where(masks[k], x, 0.0).astype(BF16), NN)
            inner = part if inner is None else inner + part
            grown.append(jnp.exp(l_col))
            tails.append(jnp.exp(last - l_col) * dt_ref[:, h : h + 1])
            shrink.append(jnp.exp(last))
        carried = contract(reads, held.astype(BF16), NN) * jnp.where(masks[0], grown[0], grown[1])
        y_ref[:, lanes] = inner + carried + x * skip_ref[:, lanes]
        scaled = (x * jnp.where(masks[0], tails[0], tails[1])).astype(BF16)
        state[:, lanes] = held * jnp.where(masks[0], shrink[0], shrink[1]) + contract(keys, scaled, TN)


def scan_backward(
    heads,
    x_ref, b_ref, c_ref, dt_ref, dtt_ref, l_ref, lt_ref, skip_ref, h_ref, dy_ref,
    dx_ref, db_ref, dc_ref, dl_ref, ddt_ref, col_ref, xdy_ref,
    d_state,
):
    @pl.when(pl.program_id(1) == 0)
    def _():
        d_state[...] = jnp.zeros_like(d_state)

    keys = b_ref[...].astype(BF16)
    reads = c_ref[...].astype(BF16)
    scores = contract(reads, keys, NT)
    lower = lower_mask()
    masks = pair_masks()
    head_lane = lax.broadcasted_iota(jnp.int32, (1, heads), 1)
    is_last = lax.broadcasted_iota(jnp.int32, (SPAN, 1), 0) == SPAN - 1
    d_scores = jnp.zeros((SPAN, SPAN), F32)
    d_keys = jnp.zeros((SPAN, STATE), F32)
    d_reads = jnp.zeros((SPAN, STATE), F32)
    d_logs = jnp.zeros((SPAN, heads), F32)
    d_steps = jnp.zeros((SPAN, heads), F32)
    x_dy = jnp.zeros((SPAN, heads), F32)
    for pair in range(heads // 2):
        lanes = slice(pair * PAIR, (pair + 1) * PAIR)
        x = x_ref[:, lanes]
        dy = dy_ref[:, lanes]
        held = h_ref[0, :, lanes]
        d_held = d_state[:, lanes]
        l_cols = [l_ref[:, 2 * pair + k : 2 * pair + k + 1] for k in range(2)]
        lasts = [l_ref[SPAN - 1 : SPAN, 2 * pair + k : 2 * pair + k + 1] for k in range(2)]
        dt_cols = [dt_ref[:, 2 * pair + k : 2 * pair + k + 1] for k in range(2)]
        rests = [jnp.exp(lasts[k] - l_cols[k]) for k in range(2)]
        shrink = [jnp.exp(lasts[k]) for k in range(2)]
        grown = jnp.where(masks[0], jnp.exp(l_cols[0]), jnp.exp(l_cols[1]))
        tails = jnp.where(masks[0], rests[0] * dt_cols[0], rests[1] * dt_cols[1])
        x_low = x.astype(BF16)
        held_low = held.astype(BF16)
        d_held_low = d_held.astype(BF16)
        outer = dy * grown
        outer_low = outer.astype(BF16)
        from_logs = outer * contract(reads, held_low, NN)
        d_reads = d_reads + contract(outer_low, held_low, NT)
        carried = contract(keys, d_held_low, NN)
        from_tails = x * carried
        d_keys = d_keys + contract((x * tails).astype(BF16), d_held_low, NT)
        x_times_dy = x * dy
        d_x = tails * carried + skip_ref[:, lanes] * dy
        kept = jnp.sum(held * d_held, axis=0, keepdims=True)
        for k in range(2):
            h = 2 * pair + k
            step_row = dtt_ref[h : h + 1, :]
            decay = jnp.exp(jnp.where(lower, l_cols[k] - lt_ref[h : h + 1, :], -1e30))
            scored = scores * decay
            dy_low = jnp.where(masks[k], dy, 0.0).astype(BF16)
            d_weights = contract(dy_low, x_low, NT)
            d_x = d_x + contract((scored * step_row).astype(BF16), dy_low, TN)
            product = d_weights * scored
            d_scores = d_scores + d_weights * decay * step_row
            col_ref[0, h : h + 1, :] = jnp.sum(product, axis=0, keepdims=True)
            row_sum = jnp.sum(product * step_row, axis=1, keepdims=True)
            log_sum = jnp.sum(jnp.where(masks[k], from_logs, 0.0), axis=1, keepdims=True)
            tail_sum = jnp.sum(jnp.where(masks[k], from_tails, 0.0), axis=1, keepdims=True)
            skip_sum = jnp.sum(jnp.where(masks[k], x_times_dy, 0.0), axis=1, keepdims=True)
            step_part = tail_sum * rests[k]
            tail_part = step_part * dt_cols[k]
            ending = shrink[k] * jnp.sum(jnp.where(masks[k], kept, 0.0), axis=1, keepdims=True) + jnp.sum(
                tail_part, axis=0, keepdims=True
            )
            log_part = log_sum + row_sum - tail_part + jnp.where(is_last, ending, 0.0)
            here = head_lane == h
            d_logs = jnp.where(here, log_part, d_logs)
            d_steps = jnp.where(here, step_part, d_steps)
            x_dy = jnp.where(here, skip_sum, x_dy)
        dx_ref[:, lanes] = d_x
        d_state[:, lanes] = d_held * jnp.where(masks[0], shrink[0], shrink[1]) + contract(reads, outer_low, TN)
    d_scores_low = d_scores.astype(BF16)
    dc_ref[...] = d_reads + contract(d_scores_low, keys, NN)
    db_ref[...] = d_keys + contract(d_scores_low, reads, TN)
    dl_ref[...] = d_logs
    ddt_ref[...] = d_steps
    xdy_ref[...] = x_dy


def scan_specs(rows, width, heads, backward):
    count = LEN // SPAN

    def at(seq, step):
        return seq * count + ((count - 1 - step) if backward else step)

    def rowwise(columns, column=0):
        return pl.BlockSpec((SPAN, columns), lambda s, i: (at(s, i), column))

    def stacked(first, second):
        return pl.BlockSpec((1, first, second), lambda s, i: (at(s, i), 0, 0))

    across = pl.BlockSpec((heads, SPAN), lambda s, i: (0, at(s, i)))
    whole = pl.BlockSpec((1, width), lambda s, i: (0, 0))
    operands = [rowwise(width), rowwise(STATE, 0), rowwise(STATE, 1), rowwise(heads), across, rowwise(heads), across, whole]
    return operands, rowwise, stacked, (rows // LEN, count)


PARAMS = pltpu.CompilerParams(
    dimension_semantics=("arbitrary", "arbitrary"), vmem_limit_bytes=40 * 1024 * 1024
)


def run_forward(x, bc, steps, logs, skip):
    rows, width = x.shape
    heads = steps.shape[1]
    operands, rowwise, stacked, grid = scan_specs(rows, width, heads, False)
    blocks = rows // SPAN
    return pl.pallas_call(
        functools.partial(scan_forward, heads),
        grid=grid,
        in_specs=operands,
        out_specs=[rowwise(width), stacked(STATE, width)],
        out_shape=[
            jax.ShapeDtypeStruct((rows, width), F32),
            jax.ShapeDtypeStruct((blocks, STATE, width), F32),
        ],
        scratch_shapes=[pltpu.VMEM((STATE, width), F32)],
        compiler_params=PARAMS,
        cost_estimate=pl.CostEstimate(
            flops=blocks * heads * 4 * SPAN * SPAN * PAIR * 4, bytes_accessed=rows * width * 10, transcendentals=blocks * heads * SPAN * SPAN
        ),
        name="scan_forward",
    )(x, bc, bc, steps, steps.T, logs, logs.T, skip)


def run_backward(x, bc, steps, logs, skip, states, d_y):
    rows, width = x.shape
    heads = steps.shape[1]
    operands, rowwise, stacked, grid = scan_specs(rows, width, heads, True)
    blocks = rows // SPAN
    return pl.pallas_call(
        functools.partial(scan_backward, heads),
        grid=grid,
        in_specs=operands + [stacked(STATE, width), rowwise(width)],
        out_specs=[
            rowwise(width), rowwise(STATE), rowwise(STATE), rowwise(heads), rowwise(heads), stacked(heads, SPAN), rowwise(heads),
        ],
        out_shape=[
            jax.ShapeDtypeStruct((rows, width), F32),
            jax.ShapeDtypeStruct((rows, STATE), F32),
            jax.ShapeDtypeStruct((rows, STATE), F32),
            jax.ShapeDtypeStruct((rows, heads), F32),
            jax.ShapeDtypeStruct((rows, heads), F32),
            jax.ShapeDtypeStruct((blocks, heads, SPAN), F32),
            jax.ShapeDtypeStruct((rows, heads), F32),
        ],
        scratch_shapes=[pltpu.VMEM((STATE, width), F32)],
        compiler_params=PARAMS,
        cost_estimate=pl.CostEstimate(
            flops=blocks * heads * 12 * SPAN * SPAN * PAIR * 4, bytes_accessed=rows * width * 20, transcendentals=blocks * heads * SPAN * SPAN
        ),
        name="scan_backward",
    )(x, bc, bc, steps, steps.T, logs, logs.T, skip, states, d_y)


def block_sums(values, reverse):
    rows, heads = values.shape
    lower = jnp.tril(jnp.ones((SPAN, SPAN), F32))
    blocks = values.reshape(rows // SPAN, SPAN, heads)
    form = "ij,cih->cjh" if reverse else "ij,cjh->cih"
    return jnp.einsum(form, lower, blocks, precision=HIGHEST).reshape(rows, heads)


def swap_mp(value, bit, size):
    return lax.ppermute(value, "mp", [(i, i ^ bit) for i in range(size)])


def gather_mp(value):
    size = lax.axis_size("mp")
    if size != 4:
        return lax.all_gather(value, "mp", axis=0, tiled=True)
    chip, core = lax.axis_index("mp") // 2, lax.axis_index("mp") % 2
    far = swap_mp(value, 2, size)
    column = jnp.stack([jnp.where(chip == 0, value, far), jnp.where(chip == 0, far, value)])
    near = swap_mp(column, 1, size)
    both = jnp.stack([jnp.where(core == 0, column, near), jnp.where(core == 0, near, column)], axis=1)
    return both.reshape((size * value.shape[0],) + value.shape[1:])


def scatter_mp(value):
    size = lax.axis_size("mp")
    if size != 4:
        return lax.psum_scatter(value, "mp", scatter_dimension=0, tiled=True)
    chip, core = lax.axis_index("mp") // 2, lax.axis_index("mp") % 2
    parts = value.reshape(2, 2, value.shape[0] // size, value.shape[1])
    near = swap_mp(lax.dynamic_index_in_dim(parts, 1 - core, 1, False).astype(BF16), 1, size)
    column = lax.dynamic_index_in_dim(parts, core, 1, False) + near.astype(F32)
    far = swap_mp(lax.dynamic_index_in_dim(column, 1 - chip, 0, False).astype(BF16), 2, size)
    return lax.dynamic_index_in_dim(column, chip, 0, False) + far.astype(F32)


def sum_all(value, axis):
    size = lax.axis_size(axis)
    bit = 1
    while bit < size:
        value = value + lax.ppermute(value, axis, [(i, i ^ bit) for i in range(size)])
        bit *= 2
    return value


def sum_parts(own, shared):
    sums = sum_all(jnp.concatenate([value.reshape(-1) for value in own + shared]), "dp")
    kept = sum(value.size for value in own)
    across = sum_all(sums[kept:], "mp")
    pieces = []
    for group, flat in ((own, sums), (shared, across)):
        place = 0
        for value in group:
            pieces.append(flat[place : place + value.size].reshape(value.shape))
            place += value.size
    return pieces


def reduce_line(parts, place, size, device):
    own = lax.dynamic_index_in_dim(parts, place, 0, False)
    for way in (1, -1):
        along = place if way == 1 else size - 1 - place
        sent = None
        for step in range(size - 1):
            target = jnp.clip(place + way * (size - 1 - step), 0, size - 1)
            part = lax.dynamic_index_in_dim(parts, target, 0, False)
            if sent is not None:
                part = part + sent.astype(F32)
            pairs = []
            for row in range(step + 1):
                here = row if way == 1 else size - 1 - row
                pairs += device(here, here + way)
            sent = lax.ppermute(part.astype(BF16), "dp", pairs)
        own = own + sent.astype(F32)
    return own


def scatter_dp(value):
    size = lax.axis_size("dp")
    if size != 8:
        return lax.psum_scatter(value, "dp", scatter_dimension=0, tiled=True)
    outer, inner = 4, 2
    parts = value.reshape(outer, inner, value.shape[0] // size, value.shape[1])
    index = lax.axis_index("dp")
    column = reduce_line(
        parts, index // inner, outer, lambda a, b: [(a * inner + i, b * inner + i) for i in range(inner)]
    )
    return reduce_line(
        column, index % inner, inner, lambda a, b: [(o * inner + a, o * inner + b) for o in range(outer)]
    )


def body(
    tokens, cotangent, in_gain, w_z, w_x, w_bc, w_dt, conv_x_w, conv_x_b, conv_bc_w, conv_bc_b, dt_bias, a_log, dskip, norm_gain, w_out,
):
    layers = w_z.shape[0]
    width = w_z.shape[2]
    heads = w_dt.shape[2]
    pair = w_bc.shape[2]
    inputs = 2 * width + pair + LANES
    pad_heads = ((0, 0), (0, LANES - heads))
    packed = []
    for depth in range(layers):
        own = jnp.concatenate(
            [w_z[depth], w_x[depth], w_bc[depth], jnp.pad(w_dt[depth], pad_heads), w_out[depth].T], axis=1
        )
        packed.append(
            tuple(lax.all_gather(part, "dp", axis=0, tiled=True) for part in (own[:, :inputs], own[:, inputs:]))
        )

    current = tokens.astype(F32)
    saved = []
    for depth in range(layers):
        w_in, w_down = packed[depth]
        scale = lax.rsqrt(jnp.mean(current * current, axis=-1, keepdims=True) + epsilon)
        normed = (current * scale * in_gain[depth]).astype(BF16)
        gathered = gather_mp(normed)
        raw = contract(gathered, w_in, NN)
        z_val = raw[:, :width]
        x_raw = raw[:, width : 2 * width]
        bc_raw = raw[:, 2 * width : 2 * width + pair]
        dt_in = raw[:, 2 * width + pair : 2 * width + pair + heads] + dt_bias[depth]
        x_act = causal_conv(x_raw, conv_x_w[depth], conv_x_b[depth])
        bc_act = causal_conv(bc_raw, conv_bc_w[depth], conv_bc_b[depth])
        steps = jax.nn.softplus(dt_in)
        rate = -jnp.exp(a_log[depth])
        logs = block_sums(steps * rate, False)
        skip = jnp.repeat(dskip[depth], HEADDIM)[None, :]
        mixed_y, states = run_forward(x_act, bc_act, steps, logs, skip)
        gated = mixed_y * jax.nn.silu(z_val)
        squares = lax.psum(jnp.sum(gated * gated, axis=-1), "mp")
        ratio = lax.rsqrt(squares / INNER + epsilon)[:, None]
        mixed = (gated * ratio * norm_gain[depth]).astype(BF16)
        branch = scatter_mp(contract(mixed, w_down, NT))
        saved.append((current, scale, gathered, raw, dt_in, x_act, bc_act, steps, rate, logs, skip, mixed_y, states, ratio, mixed))
        current = current + branch

    result = current
    gradient = cotangent.astype(F32)
    list_early, list_late, list_own, list_shared = ([], [], [], [])
    late = None
    for depth in reversed(range(layers)):
        current, scale, gathered, raw, dt_in, x_act, bc_act, steps, rate, logs, skip, mixed_y, states, ratio, mixed = saved[depth]
        w_in, w_down = packed[depth]
        z_val = raw[:, :width]
        x_raw = raw[:, width : 2 * width]
        bc_raw = raw[:, 2 * width : 2 * width + pair]
        grad_rows = gather_mp(gradient.astype(BF16))
        d_mixed = contract(grad_rows, w_down, NN)
        sigmoid_z = jax.nn.sigmoid(z_val)
        gate_act = z_val * sigmoid_z
        gated = mixed_y * gate_act
        weighted = d_mixed * norm_gain[depth]
        products = lax.psum(jnp.sum(weighted * gated, axis=-1), "mp")
        g_gain_norm = jnp.sum(d_mixed * gated * ratio, axis=0)
        d_gated = ratio * weighted - gated * ratio * ratio * ratio * (products / INNER)[:, None]
        d_y = d_gated * gate_act
        d_z = d_gated * mixed_y * sigmoid_z * (1.0 + z_val * (1.0 - sigmoid_z))
        z_low = d_z.astype(BF16)
        early = jnp.concatenate([contract(gathered, z_low, TN), contract(grad_rows, mixed, TN)], axis=1)
        d_y, early = lax.optimization_barrier((d_y, early))
        early = scatter_dp(early)
        d_x, d_keys, d_reads, d_logs, d_steps, columns, x_dy = run_backward(x_act, bc_act, steps, logs, skip, states, d_y)
        columns = jnp.swapaxes(columns, 1, 2).reshape(steps.shape)
        d_ramps = block_sums(d_logs - steps * columns, True)
        g_alog = jnp.sum(steps * d_ramps, axis=0) * rate
        d_dtr = (d_steps + columns + rate * d_ramps) * jax.nn.sigmoid(dt_in)
        g_dtb = jnp.sum(d_dtr, axis=0)
        g_skip = jnp.sum(x_dy, axis=0)
        _, x_pull = jax.vjp(causal_conv, x_raw, conv_x_w[depth], conv_x_b[depth])
        _, bc_pull = jax.vjp(causal_conv, bc_raw, conv_bc_w[depth], conv_bc_b[depth])
        d_xr, g_cxw, g_cxb = x_pull(d_x)
        d_bcr, g_cbw, g_cbb = bc_pull(jnp.concatenate([d_keys, d_reads], axis=1))
        d_low = jnp.concatenate(
            [d_xr.astype(BF16), d_bcr.astype(BF16), jnp.pad(d_dtr.astype(BF16), pad_heads)], axis=1
        )
        if late is None:
            d_low, early = lax.optimization_barrier((d_low, early))
        else:
            d_low, early, late = lax.optimization_barrier((d_low, early, late))
            list_late.append(late)
        d_normed = scatter_mp(contract(z_low, w_in[:, :width], NT) + contract(d_low, w_in[:, width:], NT))
        list_early.append(early)
        gained = d_normed * in_gain[depth]
        g_gain_in = jnp.sum(d_normed * current * scale, axis=0)
        gradient = (
            gradient
            + scale * gained
            - current * scale * scale * scale * jnp.mean(gained * current, axis=-1, keepdims=True)
        )
        if depth > 0:
            gradient, d_low = lax.optimization_barrier((gradient, d_low))
        late = scatter_dp(contract(gathered, d_low, TN))
        list_own.append(sum_parts([g_cxw, g_cxb, g_dtb, g_alog, g_skip, g_gain_norm], [g_cbw, g_cbb]))
        list_shared.append(sum_all(sum_all(g_gain_in, "dp"), "mp"))
    list_late.append(late)
    list_proj = [
        (
            early[:, :width],
            late[:, :width],
            sum_all(late[:, width : width + pair], "mp"),
            late[:, width + pair : width + pair + heads],
            early[:, width:].T,
        )
        for early, late in zip(list_early, list_late)
    ]
    proj = [jnp.stack([entry[i] for entry in list_proj[::-1]]) for i in range(5)]
    own = [jnp.stack([entry[i] for entry in list_own[::-1]]) for i in range(8)]
    g_cxw, g_cxb, g_dtb, g_alog, g_skip, g_gain_norm, g_cbw, g_cbb = own
    g_gain_in = jnp.stack(list_shared[::-1])
    return (
        result,
        gradient,
        g_gain_in,
        proj[0],
        proj[1],
        proj[2],
        proj[3],
        g_cxw,
        g_cxb,
        g_cbw,
        g_cbb,
        g_dtb,
        g_alog,
        g_skip,
        g_gain_norm,
        proj[4],
    )


def solution(mesh):
    placed = (
        P(("dp", "mp"), None),
        P(("dp", "mp"), None),
        P(),
        P(None, "dp", "mp"),
        P(None, "dp", "mp"),
        P(None, "dp", None),
        P(None, "dp", "mp"),
        P(None, None, "mp"),
        P(None, "mp"),
        P(),
        P(),
        P(None, "mp"),
        P(None, "mp"),
        P(None, "mp"),
        P(None, "mp"),
        P(None, "mp", "dp"),
    )
    return jax.shard_map(
        body,
        mesh=mesh,
        in_specs=placed,
        out_specs=placed[:1] * 2 + placed[2:],
        check_vma=False,
    )
```
